256 devices in a mesh: group: 8 (over x_hi, y), seq: 32 (over z, x_lo, core).
Axes of the slice: x: 4 (x_hi: 2, x_lo: 2; x = x_hi * 2 + x_lo), y: 4, z: 8, core: 2. Of those that a mesh axis runs over, the one named last changes fastest.
Arguments:
- queries: bfloat16 [8, 4096, 4096], P('group', 'seq'), may hold values from -100 to 100
- current_kv: bfloat16 [8, 4096, 2, 4096], P('group', 'seq'), may hold values from -5 to 5
- text_kv: bfloat16 [8, 256, 2, 4096], P('group', 'seq'), may hold values from -5 to 5
- cache_kv: bfloat16 [32, 512, 2, 4096], P('group', 'seq'), may hold values from -6 to 6
- window_ids: int32 [8, 4], replicated, may hold values from 0 to 31, as said below
- window_count: int32 [8], replicated, may hold values from 1 to 4, as said below
- cache_slot: int32 [32], replicated, may hold values from 0 to 31, as said below
- text_count: int32 [8], replicated, may hold values from 2 to 256, as said below
Outputs:
- attended: float32 [8, 4096, 4096], P('group', 'seq')
The draws below stay inside these ranges and needn't reach their ends.
Inputs may be any that keep to these rules, and one draw needn't show every extreme that they name: `window_ids`: each row names 4 different cached clips; their slots lie on exactly two indices of group (slot // 4), 2 on each. Only the first window_count[g] entries of row g are live; some clip has all 4 live and another clip only one. A permutation: cached clip c lies in slot cache_slot[c]. `text_count`: some clip uses all 256 caption tokens and another clip only two.
All inputs are finite; a program needn't handle non-finite values.
Results may differ from the reference program's by a relative error of at most 0.0013.
Values may be sent and summed in bfloat16 or wider, within the bound.
A program may use at most 64 MiB of HBM per device.

```python
import math
import jax
import jax.numpy as jnp
from jax import lax

HEADS = 32
HEAD = 128
HW = 4096
QTOK = 4096
CLIPS = 8
CACHE_TOK = 512
OWN_SLOTS = 4
SLOTS = 32
WINDOW = 4
TEXT = 256


def shared_keys(key):
    current = jnp.clip(jax.random.normal(jax.random.fold_in(key, 101), (CLIPS, QTOK, 2, HW), jnp.float32), -4.5, 4.5)
    caption = jnp.clip(jax.random.normal(jax.random.fold_in(key, 102), (CLIPS, TEXT, 2, HW), jnp.float32), -4.5, 4.5)
    return (current, caption)


def cache_plan(key):
    order = jax.random.permutation(jax.random.fold_in(key, 201), SLOTS).astype(jnp.int32)
    inverse = jnp.argsort(order).astype(jnp.int32)
    owners = SLOTS // OWN_SLOTS
    first = jax.random.randint(jax.random.fold_in(key, 202), (CLIPS,), 0, owners)
    second = (first + jax.random.randint(jax.random.fold_in(key, 203), (CLIPS,), 1, owners)) % owners
    local_a = jax.random.randint(jax.random.fold_in(key, 204), (CLIPS,), 0, OWN_SLOTS)
    local_b = (local_a + jax.random.randint(jax.random.fold_in(key, 205), (CLIPS,), 1, OWN_SLOTS)) % OWN_SLOTS
    local_c = jax.random.randint(jax.random.fold_in(key, 206), (CLIPS,), 0, OWN_SLOTS)
    local_d = (local_c + jax.random.randint(jax.random.fold_in(key, 207), (CLIPS,), 1, OWN_SLOTS)) % OWN_SLOTS
    slot_rows = jnp.stack([first * OWN_SLOTS + local_a, first * OWN_SLOTS + local_b, second * OWN_SLOTS + local_c, second * OWN_SLOTS + local_d], axis=1)
    scores = jax.random.randint(jax.random.fold_in(key, 208), (CLIPS, WINDOW), 0, 1000) * WINDOW + jnp.arange(WINDOW, dtype=jnp.int32)[None, :]
    shuffle = jnp.argsort(scores, axis=1)
    slot_rows = jnp.take_along_axis(slot_rows, shuffle, axis=1)
    return (order, inverse[slot_rows].astype(jnp.int32))


def two_rows(key):
    full_row = jax.random.randint(jax.random.fold_in(key, 1), (), 0, CLIPS)
    other_row = (full_row + jax.random.randint(jax.random.fold_in(key, 2), (), 1, CLIPS)) % CLIPS
    return (full_row, other_row)


def draw_queries(key, part):
    key = jax.random.fold_in(key, 3)
    result = 2.0 * jnp.clip(jax.random.normal(key, (CLIPS, QTOK, HW), jnp.float32), -4.5, 4.5)
    return result.astype(jnp.bfloat16)


def draw_current_kv(key, part):
    current, caption = shared_keys(key)
    return current.astype(jnp.bfloat16)


def draw_text_kv(key, part):
    current, caption = shared_keys(key)
    return caption.astype(jnp.bfloat16)


def draw_window_ids(key, part):
    order, windows = cache_plan(key)
    return windows


def draw_cache_slot(key, part):
    order, windows = cache_plan(key)
    return order


def draw_window_count(key, part):
    key = jax.random.fold_in(key, 5)
    counts = jax.random.randint(key, (CLIPS,), 1, WINDOW + 1)
    full_row, other_row = two_rows(key)
    return counts.at[full_row].set(WINDOW).at[other_row].set(1).astype(jnp.int32)


def draw_text_count(key, part):
    key = jax.random.fold_in(key, 6)
    counts = jax.random.randint(key, (CLIPS,), 2, TEXT + 1)
    full_row, other_row = two_rows(key)
    return counts.at[full_row].set(TEXT).at[other_row].set(2).astype(jnp.int32)


def levels(rng, extent, shards, low, top_value):
    level = 1.0
    for axis_at, parts in shards:
        steps = jax.random.uniform(jax.random.fold_in(jax.random.fold_in(rng, 6), axis_at), (parts,), jnp.float32, low / len(shards), top_value / len(shards))
        level = level * jnp.repeat(jnp.exp(steps), extent[axis_at] // parts).reshape((-1,) + (1,) * (len(extent) - 1 - axis_at))
    return level


def bell_draw(own_key, shape, scale, limit, shards=(), kind=jnp.bfloat16):
    drawn = jax.random.normal(own_key, shape, jnp.float32) * scale
    if len(shards) > 0:
        drawn = levels(own_key, shape, shards, -0.22, 0.18) * drawn
    return jnp.clip(drawn, min=-limit, max=limit).astype(kind)


def setup_inputs(seed: int = 0) -> dict:
    key_list = jax.random.split(jax.random.key(seed), 9)
    return {
        "queries": draw_queries(jax.random.fold_in(key_list[8], 71), 0),
        "current_kv": draw_current_kv(jax.random.fold_in(key_list[8], 71), 0),
        "text_kv": draw_text_kv(jax.random.fold_in(key_list[8], 71), 0),
        "cache_kv": bell_draw(key_list[3], (SLOTS, CACHE_TOK, 2, HW), 1.0, 6.0, ((0, 8), (1, 32))),
        "window_ids": draw_window_ids(jax.random.fold_in(key_list[8], 71), 0),
        "window_count": draw_window_count(jax.random.fold_in(key_list[8], 71), 0),
        "cache_slot": draw_cache_slot(jax.random.fold_in(key_list[8], 71), 0),
        "text_count": draw_text_count(jax.random.fold_in(key_list[8], 71), 0),
    }


def attend(query_rows, key_rows, value_rows, live_mask):
    scores = jnp.dot(query_rows, key_rows.T, preferred_element_type=jnp.float32) * (1.0 / math.sqrt(query_rows.shape[1]))
    scores = jnp.where(live_mask[None, :], scores, -1e+30)
    row_max = lax.optimization_barrier(jnp.max(scores, axis=1, keepdims=True))
    weights = jnp.exp(scores - row_max)
    row_sum = lax.optimization_barrier(jnp.sum(weights, axis=1, keepdims=True))
    weighted = jnp.dot(weights.astype(jnp.bfloat16), value_rows, preferred_element_type=jnp.float32)
    return weighted / row_sum

def reference(queries, current_kv, text_kv, cache_kv, window_ids, window_count, cache_slot, text_count):
    cache_span = WINDOW * CACHE_TOK
    entry_of_row = jnp.arange(cache_span, dtype=jnp.int32) // CACHE_TOK
    results = []
    for clip_index in range(CLIPS):
        slot_rows = cache_slot[window_ids[clip_index]]
        picked = cache_kv[slot_rows]
        key_rows = jnp.concatenate([current_kv[clip_index, :, 0], picked[:, :, 0].reshape(cache_span, HW)], axis=0)
        value_rows = jnp.concatenate([current_kv[clip_index, :, 1], picked[:, :, 1].reshape(cache_span, HW)], axis=0)
        live_mask = jnp.concatenate([jnp.ones((QTOK,), bool), entry_of_row < window_count[clip_index]])
        text_live = jnp.arange(TEXT, dtype=jnp.int32) < text_count[clip_index]
        query_all = queries[clip_index]
        text_keys = text_kv[clip_index, :, 0]
        text_values = text_kv[clip_index, :, 1]

        def per_head(head_index):
            start = head_index * HEAD
            query_head = lax.dynamic_slice_in_dim(query_all, start, HEAD, 1)
            key_head = lax.dynamic_slice_in_dim(key_rows, start, HEAD, 1)
            value_head = lax.dynamic_slice_in_dim(value_rows, start, HEAD, 1)
            tkey_head = lax.dynamic_slice_in_dim(text_keys, start, HEAD, 1)
            tvalue_head = lax.dynamic_slice_in_dim(text_values, start, HEAD, 1)
            return attend(query_head, key_head, value_head, live_mask) + attend(query_head, tkey_head, tvalue_head, text_live)
        head_out = lax.map(per_head, jnp.arange(HEADS, dtype=jnp.int32))
        results.append(head_out.transpose(1, 0, 2).reshape(QTOK, HW))
    return jnp.stack(results)
```

```python
import math

import jax
import jax.numpy as jnp
from jax import lax
from jax.experimental import pallas as pl
from jax.experimental.pallas import tpu as pltpu
from jax.sharding import PartitionSpec as P

HEAD = 128
WINDOW = 4
OWN = 4
NZ, NY = 8, 4
SEQ = 32
TOK = 128
KEYS = SEQ * TOK
CTOK = 16
CACHE = SEQ * CTOK
TTOK = 8
TEXT = SEQ * TTOK
ROWS = 512
CHUNKS = KEYS // ROWS
TILE = 512
SPAN = KEYS + WINDOW * CACHE
PARTS = 4
PART = CACHE // PARTS
SELF = 28
DEAD = -1e30
EXP_SCALE = math.log2(math.e) / math.sqrt(HEAD)
SEND_SCALE = 2.0**28
MESH = pl.DeviceIdType.MESH
BF16 = jnp.bfloat16
F32 = jnp.float32


def split_matrix(rows):
    half = rows // 2
    to = lax.broadcasted_iota(jnp.int32, (rows, rows), 0)
    at = lax.broadcasted_iota(jnp.int32, (rows, rows), 1)
    return jnp.where(at == jnp.where(to < half, 2 * to, 2 * to - rows + 1), 1.0, 0.0).astype(BF16)


def split_rows(matrix, mixed):
    return jnp.dot(matrix, mixed, preferred_element_type=F32).astype(BF16)


def body(
    q_hbm, kv_hbm, text_hbm, cache_hbm, ids, counts, slots, text_counts,
    out_hbm,
    q_raw, kv_raw, text_raw, cache_raw,
    kv_stage, cache_stage,
    q_buf, kv_buf, text_buf, text_kv,
    pool_0, pool_1, pool_2, pool_3,
    give_0, give_1, give_2, give_3,
    got_0, got_1, got_2, got_3,
    window, scores, o_buf,
    load_sem, send_sem, send_y, send_x, recv_sem, recv_q, recv_c, recv_y, recv_x,
):
    pools = (pool_0, pool_1, pool_2, pool_3)
    gives = (give_0, give_1, give_2, give_3)
    gots = (got_0, got_1, got_2, got_3)
    group = lax.axis_index("group")
    seq = lax.axis_index("seq")
    x_hi, y = group // NY, group % NY
    z, x_lo, core = seq // 4, (seq // 2) % 2, seq % 2

    def head_of(z_at, x_at, core_at):
        return z_at * 4 + ((x_at + x_hi) % 2) * 2 + core_at

    def place(step, sign):
        n = (step // 4 + 1) % NZ
        shift = (2 * (n % 2) - 1) * ((n + 1) // 2) * sign
        return (z + shift + NZ) % NZ, (x_lo + (step % 4) // 2) % 2, (core + step % 2) % 2

    def target(step, sign=1):
        z_at, x_at, core_at = place(step, sign)
        return (group, z_at * 4 + x_at * 2 + core_at)

    def columns(step):
        return pl.ds(pl.multiple_of(head_of(*place(step, 1)) * HEAD, HEAD), HEAD)

    def y_target(shift):
        return (x_hi * NY + (y + shift) % NY, seq)

    x_target = ((1 - x_hi) * NY + y, z * 4 + (1 - x_lo) * 2 + core)

    def push(src, dst, send, recv, device):
        pltpu.make_async_remote_copy(
            src_ref=src, dst_ref=dst, send_sem=send, recv_sem=recv, device_id=device, device_id_type=MESH
        ).start()

    def await_bytes(ref, sem):
        pltpu.make_async_copy(ref, ref, sem).wait()

    def each(lo, hi, fn):
        def run(step, carry):
            fn(step)
            return carry

        lax.fori_loop(lo, hi, run, 0)

    def each_remote(fn):
        each(0, SELF, fn)
        each(SELF + 1, SEQ, fn)

    loads = [
        pltpu.make_async_copy(src, dst, load_sem.at[i])
        for i, (src, dst) in enumerate(
            ((cache_hbm, cache_raw), (kv_hbm, kv_raw), (text_hbm, text_raw), (q_hbm, q_raw))
        )
    ]
    for load in loads:
        load.start()

    barrier = pltpu.get_barrier_semaphore()

    def greet(device):
        pl.semaphore_signal(barrier, inc=1, device_id=device, device_id_type=MESH)

    each_remote(lambda step: greet(target(step)))
    for shift in range(1, NY):
        greet(y_target(shift))
    greet(x_target)

    loads[0].wait()
    small = split_matrix(OWN * CTOK * 2)

    def stage_cache(step):
        mixed = cache_raw[:, :, :, columns(step)].reshape(OWN * CTOK * 2, HEAD)
        cache_stage[step] = split_rows(small, mixed).reshape(2, OWN, CTOK, HEAD)

    each(0, SEQ, stage_cache)
    pl.semaphore_wait(barrier, SEQ - 1 + NY)

    per_part = SEQ // PARTS
    for part in range(PARTS):

        def rows_of(step, part=part):
            at = pl.multiple_of((step - part * per_part) * CTOK, CTOK)
            return pools[part].at[0, :, :, pl.ds(at, CTOK), :]

        def send_cache(step, part=part):
            push(cache_stage.at[step], rows_of(step), send_sem.at[0], recv_c.at[part], target(step))

        lo, hi = part * per_part, (part + 1) * per_part
        if lo <= SELF < hi:
            pltpu.make_async_copy(cache_stage.at[SELF], rows_of(SELF), recv_c.at[part]).start()
            each(lo, SELF, send_cache)
            each(SELF + 1, hi, send_cache)
        else:
            each(lo, hi, send_cache)

    loads[1].wait()
    large = split_matrix(TOK * 2)

    def rows(step):
        return pl.ds(pl.multiple_of(step * TOK, TOK), TOK)

    def stage_kv(step):
        mixed = kv_raw[:, :, columns(step)].reshape(TOK * 2, HEAD)
        kv_stage[step] = split_rows(large, mixed).reshape(2, TOK, HEAD)

    def send_kv(step):
        stage_kv(step)
        push(kv_stage.at[step], kv_buf.at[:, rows(step), :], send_sem.at[1], recv_sem.at[1], target(step))

    each_remote(send_kv)
    stage_kv(SELF)
    pltpu.make_async_copy(kv_stage.at[SELF], kv_buf.at[:, rows(SELF), :], recv_sem.at[1]).start()

    loads[2].wait()

    def send_text(step):
        push(text_raw.at[:, :, columns(step)], text_buf.at[seq], send_sem.at[2], recv_sem.at[2], target(step))

    each_remote(send_text)
    pltpu.make_async_copy(text_raw.at[:, :, columns(SELF)], text_buf.at[seq], recv_sem.at[2]).start()

    for part in range(PARTS):
        await_bytes(pools[part].at[0], recv_c.at[part])
        for shift in range(1, NY):
            push(pools[part].at[0], pools[part].at[shift], send_y.at[part], recv_y.at[part], y_target(shift))

    loads[3].wait()

    def send_q(step):
        push(q_raw.at[:, columns(step)], q_buf.at[rows(step), :], send_sem.at[3], recv_q.at[step // 4], target(step))

    each_remote(send_q)
    pltpu.make_async_copy(
        q_raw.at[:, columns(SELF)], q_buf.at[rows(SELF), :], recv_q.at[SELF // 4]
    ).start()

    def entry(clip, w):
        slot = slots[ids[clip, w]]
        owner = slot // OWN
        return owner // NY, (y - owner % NY + NY) % NY, slot % OWN

    partner = (1 - x_hi) * NY + y
    for part in range(PARTS):
        await_bytes(pools[part].at[pl.ds(1, NY - 1)], recv_y.at[part])
        for w in range(WINDOW):
            _, shift, slot = entry(partner, w)
            gives[part][w] = pools[part][shift, :, slot]
        push(gives[part], gots[part], send_x.at[part], recv_x.at[part], x_target)

    for part in range(PARTS):
        await_bytes(gots[part], recv_x.at[part])
        for w in range(WINDOW):
            side, shift, slot = entry(group, w)
            here = jnp.full((2, PART, HEAD), side, jnp.int32) == x_hi
            near = pools[part][shift, :, slot].astype(F32)
            far = gots[part][w].astype(F32)
            window[w, :, part * PART : (part + 1) * PART, :] = jnp.where(here, near, far).astype(BF16)

    await_bytes(text_buf, recv_sem.at[2])
    for half in range(2):
        mixed = text_buf[half * 16 : (half + 1) * 16].reshape(TEXT, HEAD)
        text_kv[:, half * 128 : (half + 1) * 128, :] = split_rows(large, mixed).reshape(2, 128, HEAD)

    await_bytes(kv_buf, recv_sem.at[1])

    live = counts[group]
    biases = [jnp.where(w < live, 0.0, DEAD).astype(F32) for w in range(WINDOW)]
    text_live = lax.broadcasted_iota(jnp.int32, (ROWS, TEXT), 1) < text_counts[group]
    tiles = [(kv_buf.at[0, pl.ds(j * TILE, TILE)], kv_buf.at[1, pl.ds(j * TILE, TILE)], None) for j in range(KEYS // TILE)]
    tiles += [(window.at[w, 0], window.at[w, 1], biases[w]) for w in range(WINDOW)]

    def fold(op, wide):
        part = wide[:, 0:HEAD]
        for u in range(1, wide.shape[1] // HEAD):
            part = op(part, wide[:, u * HEAD : (u + 1) * HEAD])
        return part

    def score(q_rows, keys):
        return lax.dot_general(q_rows, keys, (((1,), (1,)), ((), ())), preferred_element_type=F32)

    ones = jnp.ones((TILE, HEAD), BF16)

    def begin(chunk):
        return q_buf[pl.ds(pl.multiple_of(chunk * ROWS, ROWS), ROWS), :]

    def first_tile(q_rows, side, j, top):
        keys, _, bias = tiles[j]
        s = score(q_rows, keys[...])
        scores[side, :, j * TILE : (j + 1) * TILE] = s
        peak = fold(jnp.maximum, s)
        if bias is not None:
            peak = peak + bias
        return peak if top is None else jnp.maximum(top, peak)

    def first_end(q_rows, side, top):
        s = jnp.where(text_live, score(q_rows, text_kv[0]), DEAD)
        scores[side, :, SPAN : SPAN + TEXT] = s
        text_top = jnp.max(fold(jnp.maximum, s), axis=1, keepdims=True)
        return jnp.max(top, axis=1, keepdims=True), text_top

    def second_tile(side, j, top, mixed):
        _, values, bias = tiles[j]
        shift = top if bias is None else top - bias
        w = jnp.exp2((scores[side, :, j * TILE : (j + 1) * TILE] - shift) * F32(EXP_SCALE))
        both = jnp.concatenate([values[...], ones], axis=1)
        return mixed + jnp.dot(w.astype(BF16), both, preferred_element_type=F32)

    def second_end(chunk, side, text_top, mixed):
        w = jnp.exp2((scores[side, :, SPAN : SPAN + TEXT] - text_top) * F32(EXP_SCALE))
        text_total = jnp.sum(fold(jnp.add, w), axis=1, keepdims=True)
        text_mixed = jnp.dot(w.astype(BF16), text_kv[1], preferred_element_type=F32)
        result = mixed[:, :HEAD] / mixed[:, HEAD:] + text_mixed / text_total
        result = result * F32(SEND_SCALE)
        result = (result * result) * (result * jnp.abs(result))
        o_buf[pl.ds(pl.multiple_of(chunk * ROWS, ROWS), ROWS), :] = result.astype(BF16)

    def advance(chunk, side, tops, follow=True):
        q_rows = begin(chunk + 1) if follow else None
        mixed = jnp.zeros((ROWS, 2 * HEAD), F32)
        top = None
        for j in range(len(tiles)):
            if follow:
                top = first_tile(q_rows, 1 - side, j, top)
            mixed = second_tile(side, j, tops[0], mixed)
        after = first_end(q_rows, 1 - side, top) if follow else None
        second_end(chunk, side, tops[1], mixed)
        return after

    my_columns = pl.ds(pl.multiple_of(head_of(z, x_lo, core) * HEAD, HEAD), HEAD)

    def send_o(step):
        push(o_buf.at[rows(step), :], out_hbm.at[:, my_columns], send_sem.at[4], recv_sem.at[4], target(step, -1))

    def q_ready(chunk):
        await_bytes(q_buf.at[pl.ds(pl.multiple_of(chunk * ROWS, ROWS), ROWS), :], recv_q.at[chunk])

    q_ready(0)
    q_rows = begin(0)
    top = None
    for j in range(len(tiles)):
        top = first_tile(q_rows, 0, j, top)
    tops = first_end(q_rows, 0, top)

    def pair(h, tops):
        for side in range(2):
            chunk = 2 * h + side
            q_ready(chunk + 1)
            tops = advance(chunk, side, tops)
            each(4 * chunk, 4 * chunk + 4, send_o)
        return tops

    tops = lax.fori_loop(0, CHUNKS // 2 - 1, pair, tops)
    q_ready(CHUNKS - 1)
    tops = advance(CHUNKS - 2, 0, tops)
    each(4 * (CHUNKS - 2), 4 * (CHUNKS - 1), send_o)
    advance(CHUNKS - 1, 1, tops, follow=False)
    pltpu.make_async_copy(o_buf.at[rows(SELF), :], out_hbm.at[:, my_columns], recv_sem.at[4]).start()
    each(SELF + 1, SEQ, send_o)

    others = pl.ds(0, SEQ - 1)
    await_bytes(cache_stage.at[others], send_sem.at[0])
    await_bytes(kv_stage.at[others], send_sem.at[1])
    await_bytes(text_buf.at[others], send_sem.at[2])
    await_bytes(q_buf.at[pl.ds(0, (SEQ - 1) * TOK), :], send_sem.at[3])
    for part in range(PARTS):
        await_bytes(pools[part].at[pl.ds(1, NY - 1)], send_y.at[part])
        await_bytes(gives[part], send_x.at[part])
    await_bytes(o_buf.at[pl.ds(0, (SEQ - 1) * TOK), :], send_sem.at[4])
    await_bytes(out_hbm, recv_sem.at[4])


def on_device(queries, current_kv, text_kv, cache_kv, window_ids, window_count, cache_slot, text_count):
    tok, width = queries.shape[1], queries.shape[2]
    hbm = pl.BlockSpec(memory_space=pl.ANY)
    smem = pl.BlockSpec(memory_space=pltpu.SMEM)
    vmem = pltpu.VMEM
    dma = pltpu.SemaphoreType.DMA
    coded = pl.pallas_call(
        body,
        out_shape=jax.ShapeDtypeStruct((tok, width), BF16),
        in_specs=[hbm] * 4 + [smem] * 4,
        out_specs=hbm,
        scratch_shapes=[
            vmem((tok, width), BF16),
            vmem((tok, 2, width), BF16),
            vmem((TTOK, 2, width), BF16),
            vmem((OWN, CTOK, 2, width), BF16),
            vmem((SEQ, 2, TOK, HEAD), BF16),
            vmem((SEQ, 2, OWN, CTOK, HEAD), BF16),
            vmem((KEYS, HEAD), BF16),
            vmem((2, KEYS, HEAD), BF16),
            vmem((SEQ, TTOK, 2, HEAD), BF16),
            vmem((2, TEXT, HEAD), BF16),
        ]
        + [vmem((NY, 2, OWN, PART, HEAD), BF16)] * PARTS
        + [vmem((WINDOW, 2, PART, HEAD), BF16)] * (2 * PARTS)
        + [
            vmem((WINDOW, 2, CACHE, HEAD), BF16),
            vmem((2, ROWS, SPAN + TEXT), F32),
            vmem((KEYS, HEAD), BF16),
            dma((4,)),
            dma((5,)),
            dma((PARTS,)),
            dma((PARTS,)),
            dma((5,)),
            dma((CHUNKS,)),
            dma((PARTS,)),
            dma((PARTS,)),
            dma((PARTS,)),
        ],
        compiler_params=pltpu.CompilerParams(
            collective_id=0, has_side_effects=True, vmem_limit_bytes=58 * 2**20
        ),
        name="attention",
    )(
        queries[0], current_kv[0], text_kv[0], cache_kv,
        window_ids, window_count, cache_slot, text_count,
    )
    coded = coded.astype(F32)
    size = jnp.sqrt(jnp.sqrt(jnp.abs(coded))) * F32(1.0 / SEND_SCALE)
    return jnp.where(coded < 0.0, -size, size).reshape(1, tok, width)


def solution(mesh):
    return jax.shard_map(
        on_device,
        mesh=mesh,
        in_specs=(
            P("group", "seq", None),
            P("group", "seq", None, None),
            P("group", "seq", None, None),
            P("group", "seq", None, None),
            P(),
            P(),
            P(),
            P(),
        ),
        out_specs=P("group", "seq", None),
        check_vma=False,
    )
```

```python
import math

import jax
import jax.numpy as jnp
from jax import lax
from jax.experimental import pallas as pl
from jax.experimental.pallas import tpu as pltpu
from jax.sharding import PartitionSpec as P

HEAD = 128
WINDOW = 4
OWN = 4
NZ, NY = 8, 4
SEQ = 32
TOK = 128
KEYS = SEQ * TOK
CTOK = 16
CACHE = SEQ * CTOK
TTOK = 8
TEXT = SEQ * TTOK
ROWS = 512
CHUNKS = KEYS // ROWS
TILE = 512
SPAN = KEYS + WINDOW * CACHE
PARTS = 4
PART = CACHE // PARTS
SELF = 28
DEAD = -1e30
EXP_SCALE = math.log2(math.e) / math.sqrt(HEAD)
SEND_SCALE = 2.0**28
MESH = pl.DeviceIdType.MESH
BF16 = jnp.bfloat16
F32 = jnp.float32


def split_matrix(rows):
    half = rows // 2
    to = lax.broadcasted_iota(jnp.int32, (rows, rows), 0)
    at = lax.broadcasted_iota(jnp.int32, (rows, rows), 1)
    return jnp.where(at == jnp.where(to < half, 2 * to, 2 * to - rows + 1), 1.0, 0.0).astype(BF16)


def split_rows(matrix, mixed):
    return jnp.dot(matrix, mixed, preferred_element_type=F32).astype(BF16)


def body(
    q_hbm, kv_hbm, text_hbm, cache_hbm, ids, counts, slots, text_counts,
    out_hbm,
    q_raw, kv_raw, text_raw, cache_raw,
    kv_stage, cache_stage,
    q_buf, kv_buf, text_buf, text_kv,
    pool_0, pool_1, pool_2, pool_3,
    give_0, give_1, give_2, give_3,
    got_0, got_1, got_2, got_3,
    window, scores, o_buf,
    load_sem, send_sem, send_y, send_x, recv_sem, recv_q, recv_c, recv_y, recv_x,
):
    pools = (pool_0, pool_1, pool_2, pool_3)
    gives = (give_0, give_1, give_2, give_3)
    gots = (got_0, got_1, got_2, got_3)
    group = lax.axis_index("group")
    seq = lax.axis_index("seq")
    x_hi, y = group // NY, group % NY
    z, x_lo, core = seq // 4, (seq // 2) % 2, seq % 2

    def head_of(z_at, x_at, core_at):
        return z_at * 4 + ((x_at + x_hi) % 2) * 2 + core_at

    def place(step, sign):
        i, q = step // 4, step % 4
        both = (i % 7 + 6) // 7
        planes = 4 - (i + 1) // 2
        shift = (1 - 2 * (q // 2) * both) * planes * sign
        dx = both * ((i + 1) % 2) + (1 - both) * (q // 2)
        return (z + shift + NZ) % NZ, (x_lo + dx) % 2, (core + q % 2) % 2

    def target(step, sign=1):
        z_at, x_at, core_at = place(step, sign)
        return (group, z_at * 4 + x_at * 2 + core_at)

    def columns(step):
        return pl.ds(pl.multiple_of(head_of(*place(step, 1)) * HEAD, HEAD), HEAD)

    def y_target(shift):
        return (x_hi * NY + (y + shift) % NY, seq)

    x_target = ((1 - x_hi) * NY + y, z * 4 + (1 - x_lo) * 2 + core)

    def push(src, dst, send, recv, device):
        pltpu.make_async_remote_copy(
            src_ref=src, dst_ref=dst, send_sem=send, recv_sem=recv, device_id=device, device_id_type=MESH
        ).start()

    def await_bytes(ref, sem):
        pltpu.make_async_copy(ref, ref, sem).wait()

    def each(lo, hi, fn):
        def run(step, carry):
            fn(step)
            return carry

        lax.fori_loop(lo, hi, run, 0)

    def each_remote(fn):
        each(0, SELF, fn)
        each(SELF + 1, SEQ, fn)

    loads = [
        pltpu.make_async_copy(src, dst, load_sem.at[i])
        for i, (src, dst) in enumerate(
            ((cache_hbm, cache_raw), (kv_hbm, kv_raw), (text_hbm, text_raw), (q_hbm, q_raw))
        )
    ]
    for i in (3, 0, 1, 2):
        loads[i].start()

    barrier = pltpu.get_barrier_semaphore()

    def greet(device):
        pl.semaphore_signal(barrier, inc=1, device_id=device, device_id_type=MESH)

    each_remote(lambda step: greet(target(step)))
    for shift in range(1, NY):
        greet(y_target(shift))
    greet(x_target)

    pl.semaphore_wait(barrier, SEQ - 1 + NY)

    def rows(step):
        return pl.ds(pl.multiple_of(step * TOK, TOK), TOK)

    def send_q(step):
        push(q_raw.at[:, columns(step)], q_buf.at[rows(step), :], send_sem.at[3], recv_q.at[step // 4], target(step))

    loads[3].wait()
    each(0, 4, send_q)

    loads[0].wait()
    small = split_matrix(OWN * CTOK * 2)

    def stage_cache(step):
        mixed = cache_raw[:, :, :, columns(step)].reshape(OWN * CTOK * 2, HEAD)
        cache_stage[step] = split_rows(small, mixed).reshape(2, OWN, CTOK, HEAD)

    per_part = SEQ // PARTS
    for part in range(PARTS):

        def rows_of(step, part=part):
            at = pl.multiple_of((step - part * per_part) * CTOK, CTOK)
            return pools[part].at[0, :, :, pl.ds(at, CTOK), :]

        def send_cache(step, part=part):
            stage_cache(step)
            push(cache_stage.at[step], rows_of(step), send_sem.at[0], recv_c.at[part], target(step))

        lo, hi = part * per_part, (part + 1) * per_part
        if lo <= SELF < hi:
            stage_cache(SELF)
            pltpu.make_async_copy(cache_stage.at[SELF], rows_of(SELF), recv_c.at[part]).start()
            each(lo, SELF, send_cache)
            each(SELF + 1, hi, send_cache)
        else:
            each(lo, hi, send_cache)

    loads[1].wait()
    large = split_matrix(TOK * 2)

    def stage_kv(step):
        mixed = kv_raw[:, :, columns(step)].reshape(TOK * 2, HEAD)
        kv_stage[step] = split_rows(large, mixed).reshape(2, TOK, HEAD)

    def send_kv(step):
        stage_kv(step)
        push(kv_stage.at[step], kv_buf.at[:, rows(step), :], send_sem.at[1], recv_sem.at[1], target(step))

    each_remote(send_kv)
    stage_kv(SELF)
    pltpu.make_async_copy(kv_stage.at[SELF], kv_buf.at[:, rows(SELF), :], recv_sem.at[1]).start()

    loads[2].wait()

    def send_text(step):
        push(text_raw.at[:, :, columns(step)], text_buf.at[seq], send_sem.at[2], recv_sem.at[2], target(step))

    each_remote(send_text)
    pltpu.make_async_copy(text_raw.at[:, :, columns(SELF)], text_buf.at[seq], recv_sem.at[2]).start()

    for part in range(PARTS):
        await_bytes(pools[part].at[0], recv_c.at[part])
        for shift in range(1, NY):
            push(pools[part].at[0], pools[part].at[shift], send_y.at[part], recv_y.at[part], y_target(shift))

    each(4, SELF, send_q)
    each(SELF + 1, SEQ, send_q)
    pltpu.make_async_copy(
        q_raw.at[:, columns(SELF)], q_buf.at[rows(SELF), :], recv_q.at[SELF // 4]
    ).start()

    def entry(clip, w):
        slot = slots[ids[w, clip]]
        owner = slot // OWN
        return owner // NY, (y - owner % NY + NY) % NY, slot % OWN

    partner = (1 - x_hi) * NY + y
    for part in range(PARTS):
        await_bytes(pools[part].at[pl.ds(1, NY - 1)], recv_y.at[part])
        for w in range(WINDOW):
            _, shift, slot = entry(partner, w)
            gives[part][w] = pools[part][shift, :, slot]
        push(gives[part], gots[part], send_x.at[part], recv_x.at[part], x_target)

    for part in range(PARTS):
        await_bytes(gots[part], recv_x.at[part])
        for w in range(WINDOW):
            side, shift, slot = entry(group, w)
            here = jnp.full((2, PART, HEAD), side, jnp.int32) == x_hi
            near = pools[part][shift, :, slot].astype(F32)
            far = gots[part][w].astype(F32)
            window[w, :, part * PART : (part + 1) * PART, :] = jnp.where(here, near, far).astype(BF16)

    await_bytes(text_buf, recv_sem.at[2])
    for half in range(2):
        mixed = text_buf[half * 16 : (half + 1) * 16].reshape(TEXT, HEAD)
        text_kv[:, half * 128 : (half + 1) * 128, :] = split_rows(large, mixed).reshape(2, 128, HEAD)

    await_bytes(kv_buf, recv_sem.at[1])

    live = counts[group]
    biases = [jnp.where(w < live, 0.0, DEAD).astype(F32) for w in range(WINDOW)]
    text_live = lax.broadcasted_iota(jnp.int32, (ROWS, TEXT), 1) < text_counts[group]
    tiles = [(kv_buf.at[0, pl.ds(j * TILE, TILE)], kv_buf.at[1, pl.ds(j * TILE, TILE)], None) for j in range(KEYS // TILE)]
    tiles += [(window.at[w, 0], window.at[w, 1], biases[w]) for w in range(WINDOW)]

    def fold(op, wide):
        part = wide[:, 0:HEAD]
        for u in range(1, wide.shape[1] // HEAD):
            part = op(part, wide[:, u * HEAD : (u + 1) * HEAD])
        return part

    def score(q_rows, keys):
        return lax.dot_general(q_rows, keys, (((1,), (1,)), ((), ())), preferred_element_type=F32)

    ones = jnp.ones((TILE, HEAD), BF16)

    def begin(chunk):
        return q_buf[pl.ds(pl.multiple_of(chunk * ROWS, ROWS), ROWS), :]

    def first_tile(q_rows, side, j, top):
        keys, _, bias = tiles[j]
        s = score(q_rows, keys[...])
        scores[side, :, j * TILE : (j + 1) * TILE] = s
        peak = fold(jnp.maximum, s)
        if bias is not None:
            peak = peak + bias
        return peak if top is None else jnp.maximum(top, peak)

    def first_end(q_rows, side, top):
        s = jnp.where(text_live, score(q_rows, text_kv[0]), DEAD)
        scores[side, :, SPAN : SPAN + TEXT] = s
        text_top = jnp.max(fold(jnp.maximum, s), axis=1, keepdims=True)
        return jnp.max(top, axis=1, keepdims=True), text_top

    def second_tile(side, j, top, mixed):
        _, values, bias = tiles[j]
        shift = top if bias is None else top - bias
        w = jnp.exp2((scores[side, :, j * TILE : (j + 1) * TILE] - shift) * F32(EXP_SCALE))
        both = jnp.concatenate([values[...], ones], axis=1)
        return mixed + jnp.dot(w.astype(BF16), both, preferred_element_type=F32)

    def second_end(chunk, side, text_top, mixed):
        w = jnp.exp2((scores[side, :, SPAN : SPAN + TEXT] - text_top) * F32(EXP_SCALE))
        text_total = jnp.sum(fold(jnp.add, w), axis=1, keepdims=True)
        text_mixed = jnp.dot(w.astype(BF16), text_kv[1], preferred_element_type=F32)
        result = mixed[:, :HEAD] / mixed[:, HEAD:] + text_mixed / text_total
        result = result * F32(SEND_SCALE)
        result = (result * result) * (result * jnp.abs(result))
        o_buf[pl.ds(pl.multiple_of(chunk * ROWS, ROWS), ROWS), :] = result.astype(BF16)

    def advance(chunk, side, tops, follow=True):
        q_rows = begin(chunk + 1) if follow else None
        mixed = jnp.zeros((ROWS, 2 * HEAD), F32)
        top = None
        for j in range(len(tiles)):
            if follow:
                top = first_tile(q_rows, 1 - side, j, top)
            mixed = second_tile(side, j, tops[0], mixed)
        after = first_end(q_rows, 1 - side, top) if follow else None
        second_end(chunk, side, tops[1], mixed)
        return after

    my_columns = pl.ds(pl.multiple_of(head_of(z, x_lo, core) * HEAD, HEAD), HEAD)

    def send_o(step):
        push(o_buf.at[rows(step), :], out_hbm.at[:, my_columns], send_sem.at[4], recv_sem.at[4], target(step, -1))

    def q_ready(chunk):
        await_bytes(q_buf.at[pl.ds(pl.multiple_of(chunk * ROWS, ROWS), ROWS), :], recv_q.at[chunk])

    q_ready(0)
    q_rows = begin(0)
    top = None
    for j in range(len(tiles)):
        top = first_tile(q_rows, 0, j, top)
    tops = first_end(q_rows, 0, top)

    def pair(h, tops):
        for side in range(2):
            chunk = 2 * h + side
            q_ready(chunk + 1)
            tops = advance(chunk, side, tops)
            each(4 * chunk, 4 * chunk + 4, send_o)
        return tops

    tops = lax.fori_loop(0, CHUNKS // 2 - 1, pair, tops)
    q_ready(CHUNKS - 1)
    tops = advance(CHUNKS - 2, 0, tops)
    each(4 * (CHUNKS - 2), 4 * (CHUNKS - 1), send_o)
    advance(CHUNKS - 1, 1, tops, follow=False)
    pltpu.make_async_copy(o_buf.at[rows(SELF), :], out_hbm.at[:, my_columns], recv_sem.at[4]).start()
    each(SELF + 1, SEQ, send_o)

    others = pl.ds(0, SEQ - 1)
    await_bytes(cache_stage.at[others], send_sem.at[0])
    await_bytes(kv_stage.at[others], send_sem.at[1])
    await_bytes(text_buf.at[others], send_sem.at[2])
    await_bytes(q_buf.at[pl.ds(0, (SEQ - 1) * TOK), :], send_sem.at[3])
    for part in range(PARTS):
        await_bytes(pools[part].at[pl.ds(1, NY - 1)], send_y.at[part])
        await_bytes(gives[part], send_x.at[part])
    await_bytes(o_buf.at[pl.ds(0, (SEQ - 1) * TOK), :], send_sem.at[4])
    await_bytes(out_hbm, recv_sem.at[4])


def on_device(queries, current_kv, text_kv, cache_kv, window_ids, window_count, cache_slot, text_count):
    tok, width = queries.shape[1], queries.shape[2]
    hbm = pl.BlockSpec(memory_space=pl.ANY)
    smem = pl.BlockSpec(memory_space=pltpu.SMEM)
    vmem = pltpu.VMEM
    dma = pltpu.SemaphoreType.DMA
    coded = pl.pallas_call(
        body,
        out_shape=jax.ShapeDtypeStruct((tok, width), BF16),
        in_specs=[hbm] * 4 + [smem] * 4,
        out_specs=hbm,
        scratch_shapes=[
            vmem((tok, width), BF16),
            vmem((tok, 2, width), BF16),
            vmem((TTOK, 2, width), BF16),
            vmem((OWN, CTOK, 2, width), BF16),
            vmem((SEQ, 2, TOK, HEAD), BF16),
            vmem((SEQ, 2, OWN, CTOK, HEAD), BF16),
            vmem((KEYS, HEAD), BF16),
            vmem((2, KEYS, HEAD), BF16),
            vmem((SEQ, TTOK, 2, HEAD), BF16),
            vmem((2, TEXT, HEAD), BF16),
        ]
        + [vmem((NY, 2, OWN, PART, HEAD), BF16)] * PARTS
        + [vmem((WINDOW, 2, PART, HEAD), BF16)] * (2 * PARTS)
        + [
            vmem((WINDOW, 2, CACHE, HEAD), BF16),
            vmem((2, ROWS, SPAN + TEXT), F32),
            vmem((KEYS, HEAD), BF16),
            dma((4,)),
            dma((5,)),
            dma((PARTS,)),
            dma((PARTS,)),
            dma((5,)),
            dma((CHUNKS,)),
            dma((PARTS,)),
            dma((PARTS,)),
            dma((PARTS,)),
        ],
        compiler_params=pltpu.CompilerParams(
            collective_id=0, has_side_effects=True, vmem_limit_bytes=58 * 2**20
        ),
        name="attention",
    )(
        queries[0], current_kv[0], text_kv[0], cache_kv,
        window_ids.T, window_count, cache_slot, text_count,
    )
    coded = coded.astype(F32)
    size = lax.rsqrt(lax.rsqrt(jnp.abs(coded))) * F32(1.0 / SEND_SCALE)
    return jnp.where(coded < 0.0, -size, size).reshape(1, tok, width)


def solution(mesh):
    return jax.shard_map(
        on_device,
        mesh=mesh,
        in_specs=(
            P("group", "seq", None),
            P("group", "seq", None, None),
            P("group", "seq", None, None),
            P("group", "seq", None, None),
            P(),
            P(),
            P(),
            P(),
        ),
        out_specs=P("group", "seq", None),
        check_vma=False,
    )
```

```python
import math

import jax
import jax.numpy as jnp
from jax import lax
from jax.experimental import pallas as pl
from jax.experimental.pallas import tpu as pltpu
from jax.sharding import PartitionSpec as P

HEAD = 128
WINDOW = 4
OWN = 4
NZ, NY = 8, 4
SEQ = 32
TOK = 128
KEYS = SEQ * TOK
CTOK = 16
CACHE = SEQ * CTOK
TTOK = 8
TEXT = SEQ * TTOK
ROWS = 512
CHUNKS = KEYS // ROWS
TILE = 512
SPAN = KEYS + WINDOW * CACHE
PARTS = 4
PART = CACHE // PARTS
SELF = 4
DEAD = -1e30
EXP_SCALE = math.log2(math.e) / math.sqrt(HEAD)
SEND_SCALE = 2.0**28
MESH = pl.DeviceIdType.MESH
BF16 = jnp.bfloat16
F32 = jnp.float32


def split_matrix(rows):
    half = rows // 2
    to = lax.broadcasted_iota(jnp.int32, (rows, rows), 0)
    at = lax.broadcasted_iota(jnp.int32, (rows, rows), 1)
    return jnp.where(at == jnp.where(to < half, 2 * to, 2 * to - rows + 1), 1.0, 0.0).astype(BF16)


def split_rows(matrix, mixed):
    return jnp.dot(matrix, mixed, preferred_element_type=F32).astype(BF16)


def body(
    q_hbm, kv_hbm, text_hbm, cache_hbm, ids, counts, slots, text_counts,
    out_hbm,
    q_raw, kv_raw, text_raw, cache_raw,
    kv_stage, cache_stage,
    q_buf, kv_buf, text_buf, text_kv,
    pool_0, pool_1, pool_2, pool_3,
    give_0, give_1, give_2, give_3,
    got_0, got_1, got_2, got_3,
    window, scores, o_buf,
    load_sem, send_sem, send_y, send_x, recv_sem, recv_kv, recv_q, recv_c, recv_y, recv_x,
):
    pools = (pool_0, pool_1, pool_2, pool_3)
    gives = (give_0, give_1, give_2, give_3)
    gots = (got_0, got_1, got_2, got_3)
    group = lax.axis_index("group")
    seq = lax.axis_index("seq")
    x_hi, y = group // NY, group % NY
    z, x_lo, core = seq // 4, (seq // 2) % 2, seq % 2

    def head_of(z_at, x_at, core_at):
        return z_at * 4 + ((x_at + x_hi) % 2) * 2 + core_at

    def place(step, sign):
        i, q = (step // 4 + 6) % 8, step % 4
        both = (i % 7 + 6) // 7
        planes = 4 - (i + 1) // 2
        shift = (1 - 2 * (q // 2) * both) * planes * sign
        dx = both * ((i + 1) % 2) + (1 - both) * (q // 2)
        return (z + shift + NZ) % NZ, (x_lo + dx) % 2, (core + q % 2) % 2

    def target(step, sign=1):
        z_at, x_at, core_at = place(step, sign)
        return (group, z_at * 4 + x_at * 2 + core_at)

    def columns(step):
        return pl.ds(pl.multiple_of(head_of(*place(step, 1)) * HEAD, HEAD), HEAD)

    def y_target(shift):
        return (x_hi * NY + (y + shift) % NY, seq)

    x_target = ((1 - x_hi) * NY + y, z * 4 + (1 - x_lo) * 2 + core)

    def push(src, dst, send, recv, device):
        pltpu.make_async_remote_copy(
            src_ref=src, dst_ref=dst, send_sem=send, recv_sem=recv, device_id=device, device_id_type=MESH
        ).start()

    def await_bytes(ref, sem):
        pltpu.make_async_copy(ref, ref, sem).wait()

    def each(lo, hi, fn):
        def run(step, carry):
            fn(step)
            return carry

        lax.fori_loop(lo, hi, run, 0)

    def each_remote(fn):
        each(0, SELF, fn)
        each(SELF + 1, SEQ, fn)

    loads = [
        pltpu.make_async_copy(src, dst, load_sem.at[i])
        for i, (src, dst) in enumerate(
            ((cache_hbm, cache_raw), (kv_hbm, kv_raw), (text_hbm, text_raw), (q_hbm, q_raw))
        )
    ]
    for i in (3, 0, 1, 2):
        loads[i].start()

    barrier = pltpu.get_barrier_semaphore()

    def greet(device):
        pl.semaphore_signal(barrier, inc=1, device_id=device, device_id_type=MESH)

    each_remote(lambda step: greet(target(step)))
    for shift in range(1, NY):
        greet(y_target(shift))
    greet(x_target)

    pl.semaphore_wait(barrier, SEQ - 1 + NY)

    def rows(step):
        return pl.ds(pl.multiple_of(step * TOK, TOK), TOK)

    def send_q(step):
        push(q_raw.at[:, columns(step)], q_buf.at[rows(step), :], send_sem.at[3], recv_q.at[step // 4], target(step))

    loads[3].wait()
    each(0, SELF, send_q)
    each(SELF + 1, 8, send_q)
    pltpu.make_async_copy(
        q_raw.at[:, columns(SELF)], q_buf.at[rows(SELF), :], recv_q.at[SELF // 4]
    ).start()

    loads[0].wait()
    small = split_matrix(OWN * CTOK * 2)

    def stage_cache(step):
        mixed = cache_raw[:, :, :, columns(step)].reshape(OWN * CTOK * 2, HEAD)
        cache_stage[step] = split_rows(small, mixed).reshape(2, OWN, CTOK, HEAD)

    per_part = SEQ // PARTS
    for part in range(PARTS):

        def rows_of(step, part=part):
            at = pl.multiple_of((step - part * per_part) * CTOK, CTOK)
            return pools[part].at[0, :, :, pl.ds(at, CTOK), :]

        def send_cache(step, part=part):
            stage_cache(step)
            push(cache_stage.at[step], rows_of(step), send_sem.at[0], recv_c.at[part], target(step))

        lo, hi = part * per_part, (part + 1) * per_part
        if lo <= SELF < hi:
            stage_cache(SELF)
            pltpu.make_async_copy(cache_stage.at[SELF], rows_of(SELF), recv_c.at[part]).start()
            each(lo, SELF, send_cache)
            each(SELF + 1, hi, send_cache)
        else:
            each(lo, hi, send_cache)

    loads[2].wait()

    def send_text(step):
        push(text_raw.at[:, :, columns(step)], text_buf.at[seq], send_sem.at[2], recv_sem.at[2], target(step))

    each_remote(send_text)
    pltpu.make_async_copy(text_raw.at[:, :, columns(SELF)], text_buf.at[seq], recv_sem.at[2]).start()

    loads[1].wait()
    large = split_matrix(TOK * 2)

    def stage_kv(step):
        mixed = kv_raw[:, :, columns(step)].reshape(TOK * 2, HEAD)
        kv_stage[step] = split_rows(large, mixed).reshape(2, TOK, HEAD)

    def send_kv(step, kind):
        push(kv_stage.at[step, kind], kv_buf.at[kind, rows(step), :], send_sem.at[1], recv_kv.at[kind], target(step))

    def send_keys(step):
        stage_kv(step)
        send_kv(step, 0)

    each_remote(send_keys)
    stage_kv(SELF)
    for kind in range(2):
        pltpu.make_async_copy(
            kv_stage.at[SELF, kind], kv_buf.at[kind, rows(SELF), :], recv_kv.at[kind]
        ).start()
    each_remote(lambda step: send_kv(step, 1))

    for part in range(PARTS):
        await_bytes(pools[part].at[0], recv_c.at[part])
        for shift in range(1, NY):
            push(pools[part].at[0], pools[part].at[shift], send_y.at[part], recv_y.at[part], y_target(shift))

    each(8, SEQ, send_q)

    def entry(clip, w):
        slot = slots[ids[w, clip]]
        owner = slot // OWN
        return owner // NY, (y - owner % NY + NY) % NY, slot % OWN

    partner = (1 - x_hi) * NY + y
    for part in range(PARTS):
        await_bytes(pools[part].at[pl.ds(1, NY - 1)], recv_y.at[part])
        for w in range(WINDOW):
            _, shift, slot = entry(partner, w)
            gives[part][w] = pools[part][shift, :, slot]
        push(gives[part], gots[part], send_x.at[part], recv_x.at[part], x_target)

    for part in range(PARTS):
        await_bytes(gots[part], recv_x.at[part])
        for w in range(WINDOW):
            side, shift, slot = entry(group, w)
            here = jnp.full((2, PART, HEAD), side, jnp.int32) == x_hi
            near = pools[part][shift, :, slot].astype(F32)
            far = gots[part][w].astype(F32)
            window[w, :, part * PART : (part + 1) * PART, :] = jnp.where(here, near, far).astype(BF16)

    await_bytes(text_buf, recv_sem.at[2])
    for half in range(2):
        mixed = text_buf[half * 16 : (half + 1) * 16].reshape(TEXT, HEAD)
        text_kv[:, half * 128 : (half + 1) * 128, :] = split_rows(large, mixed).reshape(2, 128, HEAD)

    await_bytes(kv_buf.at[0], recv_kv.at[0])

    live = counts[group]
    biases = [jnp.where(w < live, 0.0, DEAD).astype(F32) for w in range(WINDOW)]
    text_live = lax.broadcasted_iota(jnp.int32, (ROWS, TEXT), 1) < text_counts[group]
    tiles = [(kv_buf.at[0, pl.ds(j * TILE, TILE)], kv_buf.at[1, pl.ds(j * TILE, TILE)], None) for j in range(KEYS // TILE)]
    tiles += [(window.at[w, 0], window.at[w, 1], biases[w]) for w in range(WINDOW)]

    def fold(op, wide):
        part = wide[:, 0:HEAD]
        for u in range(1, wide.shape[1] // HEAD):
            part = op(part, wide[:, u * HEAD : (u + 1) * HEAD])
        return part

    def score(q_rows, keys):
        return lax.dot_general(q_rows, keys, (((1,), (1,)), ((), ())), preferred_element_type=F32)

    ones = jnp.ones((TILE, HEAD), BF16)

    def begin(chunk):
        return q_buf[pl.ds(pl.multiple_of(chunk * ROWS, ROWS), ROWS), :]

    def first_tile(q_rows, side, j, top):
        keys, _, bias = tiles[j]
        s = score(q_rows, keys[...])
        scores[side, :, j * TILE : (j + 1) * TILE] = s
        peak = fold(jnp.maximum, s)
        if bias is not None:
            peak = peak + bias
        return peak if top is None else jnp.maximum(top, peak)

    def first_end(q_rows, side, top):
        s = jnp.where(text_live, score(q_rows, text_kv[0]), DEAD)
        scores[side, :, SPAN : SPAN + TEXT] = s
        text_top = jnp.max(fold(jnp.maximum, s), axis=1, keepdims=True)
        return jnp.max(top, axis=1, keepdims=True), text_top

    def second_tile(side, j, top, mixed):
        _, values, bias = tiles[j]
        shift = top if bias is None else top - bias
        w = jnp.exp2((scores[side, :, j * TILE : (j + 1) * TILE] - shift) * F32(EXP_SCALE))
        both = jnp.concatenate([values[...], ones], axis=1)
        return mixed + jnp.dot(w.astype(BF16), both, preferred_element_type=F32)

    def second_end(chunk, side, text_top, mixed):
        w = jnp.exp2((scores[side, :, SPAN : SPAN + TEXT] - text_top) * F32(EXP_SCALE))
        text_total = jnp.sum(fold(jnp.add, w), axis=1, keepdims=True)
        text_mixed = jnp.dot(w.astype(BF16), text_kv[1], preferred_element_type=F32)
        result = mixed[:, :HEAD] / mixed[:, HEAD:] + text_mixed / text_total
        result = result * F32(SEND_SCALE)
        result = (result * result) * (result * jnp.abs(result))
        o_buf[pl.ds(pl.multiple_of(chunk * ROWS, ROWS), ROWS), :] = result.astype(BF16)

    def advance(chunk, side, tops, follow=True):
        q_rows = begin(chunk + 1) if follow else None
        mixed = jnp.zeros((ROWS, 2 * HEAD), F32)
        top = None
        for j in range(len(tiles)):
            if follow:
                top = first_tile(q_rows, 1 - side, j, top)
            mixed = second_tile(side, j, tops[0], mixed)
        after = first_end(q_rows, 1 - side, top) if follow else None
        second_end(chunk, side, tops[1], mixed)
        return after

    my_columns = pl.ds(pl.multiple_of(head_of(z, x_lo, core) * HEAD, HEAD), HEAD)

    def send_o(step):
        push(o_buf.at[rows(step), :], out_hbm.at[:, my_columns], send_sem.at[4], recv_sem.at[4], target(step, -1))

    def q_ready(chunk):
        await_bytes(q_buf.at[pl.ds(pl.multiple_of(chunk * ROWS, ROWS), ROWS), :], recv_q.at[chunk])

    q_ready(0)
    q_rows = begin(0)
    top = None
    for j in range(len(tiles)):
        top = first_tile(q_rows, 0, j, top)
    tops = first_end(q_rows, 0, top)

    def send_chunk(chunk):
        own = jnp.where(chunk == SELF // 4, 1, 0)
        each(4 * chunk + own, 4 * chunk + 4, send_o)

        @pl.when(chunk == SELF // 4)
        def _():
            pltpu.make_async_copy(o_buf.at[rows(SELF), :], out_hbm.at[:, my_columns], recv_sem.at[4]).start()

    def pair(h, tops):
        for side in range(2):
            chunk = 2 * h + side
            q_ready(chunk + 1)
            tops = advance(chunk, side, tops)
            send_chunk(chunk)
        return tops

    await_bytes(kv_buf.at[1], recv_kv.at[1])
    tops = lax.fori_loop(0, CHUNKS // 2 - 1, pair, tops)
    q_ready(CHUNKS - 1)
    tops = advance(CHUNKS - 2, 0, tops)
    each(4 * (CHUNKS - 2), 4 * (CHUNKS - 1), send_o)
    advance(CHUNKS - 1, 1, tops, follow=False)
    each(4 * (CHUNKS - 1), SEQ, send_o)

    others = pl.ds(0, SEQ - 1)
    await_bytes(cache_stage.at[others], send_sem.at[0])
    await_bytes(kv_stage.at[others], send_sem.at[1])
    await_bytes(text_buf.at[others], send_sem.at[2])
    await_bytes(q_buf.at[pl.ds(0, (SEQ - 1) * TOK), :], send_sem.at[3])
    for part in range(PARTS):
        await_bytes(pools[part].at[pl.ds(1, NY - 1)], send_y.at[part])
        await_bytes(gives[part], send_x.at[part])
    await_bytes(o_buf.at[pl.ds(0, (SEQ - 1) * TOK), :], send_sem.at[4])
    await_bytes(out_hbm, recv_sem.at[4])


def on_device(queries, current_kv, text_kv, cache_kv, window_ids, window_count, cache_slot, text_count):
    tok, width = queries.shape[1], queries.shape[2]
    hbm = pl.BlockSpec(memory_space=pl.ANY)
    smem = pl.BlockSpec(memory_space=pltpu.SMEM)
    vmem = pltpu.VMEM
    dma = pltpu.SemaphoreType.DMA
    coded = pl.pallas_call(
        body,
        out_shape=jax.ShapeDtypeStruct((tok, width), BF16),
        in_specs=[hbm] * 4 + [smem] * 4,
        out_specs=hbm,
        scratch_shapes=[
            vmem((tok, width), BF16),
            vmem((tok, 2, width), BF16),
            vmem((TTOK, 2, width), BF16),
            vmem((OWN, CTOK, 2, width), BF16),
            vmem((SEQ, 2, TOK, HEAD), BF16),
            vmem((SEQ, 2, OWN, CTOK, HEAD), BF16),
            vmem((KEYS, HEAD), BF16),
            vmem((2, KEYS, HEAD), BF16),
            vmem((SEQ, TTOK, 2, HEAD), BF16),
            vmem((2, TEXT, HEAD), BF16),
        ]
        + [vmem((NY, 2, OWN, PART, HEAD), BF16)] * PARTS
        + [vmem((WINDOW, 2, PART, HEAD), BF16)] * (2 * PARTS)
        + [
            vmem((WINDOW, 2, CACHE, HEAD), BF16),
            vmem((2, ROWS, SPAN + TEXT), F32),
            vmem((KEYS, HEAD), BF16),
            dma((4,)),
            dma((5,)),
            dma((PARTS,)),
            dma((PARTS,)),
            dma((5,)),
            dma((2,)),
            dma((CHUNKS,)),
            dma((PARTS,)),
            dma((PARTS,)),
            dma((PARTS,)),
        ],
        compiler_params=pltpu.CompilerParams(
            collective_id=0, has_side_effects=True, vmem_limit_bytes=58 * 2**20
        ),
        name="attention",
    )(
        queries[0], current_kv[0], text_kv[0], cache_kv,
        window_ids.T, window_count, cache_slot, text_count,
    )
    coded = coded.astype(F32)
    size = lax.rsqrt(lax.rsqrt(jnp.abs(coded))) * F32(1.0 / SEND_SCALE)
    return jnp.where(coded < 0.0, -size, size).reshape(1, tok, width)


def solution(mesh):
    return jax.shard_map(
        on_device,
        mesh=mesh,
        in_specs=(
            P("group", "seq", None),
            P("group", "seq", None, None),
            P("group", "seq", None, None),
            P("group", "seq", None, None),
            P(),
            P(),
            P(),
            P(),
        ),
        out_specs=P("group", "seq", None),
        check_vma=False,
    )
```

```python
import math

import jax
import jax.numpy as jnp
from jax import lax
from jax.experimental import pallas as pl
from jax.experimental.pallas import tpu as pltpu
from jax.sharding import PartitionSpec as P

HEAD = 128
WINDOW = 4
OWN = 4
NZ, NY = 8, 4
SEQ = 32
TOK = 128
KEYS = SEQ * TOK
CTOK = 16
CACHE = SEQ * CTOK
TTOK = 8
TEXT = SEQ * TTOK
ROWS = 512
CHUNKS = KEYS // ROWS
TILE = 512
SPAN = KEYS + WINDOW * CACHE
PARTS = 4
PART = CACHE // PARTS
SELF = 4
PIECES = 4
PIECE = TOK // PIECES
DEAD = -1e30
EXP_SCALE = math.log2(math.e) / math.sqrt(HEAD)
SEND_SCALE = 2.0**28
MESH = pl.DeviceIdType.MESH
BF16 = jnp.bfloat16
F32 = jnp.float32


def split_matrix(rows):
    half = rows // 2
    to = lax.broadcasted_iota(jnp.int32, (rows, rows), 0)
    at = lax.broadcasted_iota(jnp.int32, (rows, rows), 1)
    return jnp.where(at == jnp.where(to < half, 2 * to, 2 * to - rows + 1), 1.0, 0.0).astype(BF16)


def split_rows(matrix, mixed):
    return jnp.dot(matrix, mixed, preferred_element_type=F32).astype(BF16)


def body(
    q_hbm, kv_hbm, text_hbm, cache_hbm, ids, counts, slots, text_counts,
    out_hbm,
    q_raw, kv_raw, text_raw, cache_raw,
    kv_stage, cache_stage,
    q_buf, kv_buf, text_buf, text_kv,
    pool_0, pool_1, pool_2, pool_3,
    give_0, give_1, give_2, give_3,
    got_0, got_1, got_2, got_3,
    window, scores, o_buf,
    load_sem, send_sem, send_y, send_x, recv_sem, recv_kv, recv_q, recv_c, recv_y, recv_x,
):
    pools = (pool_0, pool_1, pool_2, pool_3)
    gives = (give_0, give_1, give_2, give_3)
    gots = (got_0, got_1, got_2, got_3)
    group = lax.axis_index("group")
    seq = lax.axis_index("seq")
    x_hi, y = group // NY, group % NY
    z, x_lo, core = seq // 4, (seq // 2) % 2, seq % 2

    def head_of(z_at, x_at, core_at):
        return z_at * 4 + ((x_at + x_hi) % 2) * 2 + core_at

    def place(step, sign):
        i, q = (step // 4 + 6) % 8, step % 4
        both = (i % 7 + 6) // 7
        planes = 4 - (i + 1) // 2
        shift = (1 - 2 * (q // 2) * both) * planes * sign
        dx = both * ((i + 1) % 2) + (1 - both) * (q // 2)
        return (z + shift + NZ) % NZ, (x_lo + dx) % 2, (core + q % 2) % 2

    def target(step, sign=1):
        z_at, x_at, core_at = place(step, sign)
        return (group, z_at * 4 + x_at * 2 + core_at)

    def columns(step):
        return pl.ds(pl.multiple_of(head_of(*place(step, 1)) * HEAD, HEAD), HEAD)

    def y_target(shift):
        return (x_hi * NY + (y + shift) % NY, seq)

    x_target = ((1 - x_hi) * NY + y, z * 4 + (1 - x_lo) * 2 + core)

    def push(src, dst, send, recv, device):
        pltpu.make_async_remote_copy(
            src_ref=src, dst_ref=dst, send_sem=send, recv_sem=recv, device_id=device, device_id_type=MESH
        ).start()

    def await_bytes(ref, sem):
        pltpu.make_async_copy(ref, ref, sem).wait()

    def each(lo, hi, fn):
        def run(step, carry):
            fn(step)
            return carry

        lax.fori_loop(lo, hi, run, 0)

    def each_remote(fn):
        each(0, SELF, fn)
        each(SELF + 1, SEQ, fn)

    loads = [
        pltpu.make_async_copy(src, dst, load_sem.at[i])
        for i, (src, dst) in enumerate(
            ((cache_hbm, cache_raw), (kv_hbm, kv_raw), (text_hbm, text_raw), (q_hbm, q_raw))
        )
    ]
    for i in (3, 0, 1, 2):
        loads[i].start()

    barrier = pltpu.get_barrier_semaphore()

    def greet(device):
        pl.semaphore_signal(barrier, inc=1, device_id=device, device_id_type=MESH)

    each_remote(lambda step: greet(target(step)))
    for shift in range(1, NY):
        greet(y_target(shift))
    greet(x_target)

    pl.semaphore_wait(barrier, SEQ - 1 + NY)

    def rows(step):
        return pl.ds(pl.multiple_of(step * TOK, TOK), TOK)

    def send_q(step):
        push(q_raw.at[:, columns(step)], q_buf.at[rows(step), :], send_sem.at[3], recv_q.at[step // 4], target(step))

    loads[3].wait()
    each(0, SELF, send_q)
    each(SELF + 1, 8, send_q)
    pltpu.make_async_copy(
        q_raw.at[:, columns(SELF)], q_buf.at[rows(SELF), :], recv_q.at[SELF // 4]
    ).start()

    loads[0].wait()
    small = split_matrix(OWN * CTOK * 2)

    def stage_cache(step):
        mixed = cache_raw[:, :, :, columns(step)].reshape(OWN * CTOK * 2, HEAD)
        cache_stage[step] = split_rows(small, mixed).reshape(2, OWN, CTOK, HEAD)

    per_part = SEQ // PARTS
    for part in range(PARTS):

        def rows_of(step, part=part):
            at = pl.multiple_of((step - part * per_part) * CTOK, CTOK)
            return pools[part].at[0, :, :, pl.ds(at, CTOK), :]

        def send_cache(step, part=part):
            stage_cache(step)
            push(cache_stage.at[step], rows_of(step), send_sem.at[0], recv_c.at[part], target(step))

        lo, hi = part * per_part, (part + 1) * per_part
        if lo <= SELF < hi:
            stage_cache(SELF)
            pltpu.make_async_copy(cache_stage.at[SELF], rows_of(SELF), recv_c.at[part]).start()
            each(lo, SELF, send_cache)
            each(SELF + 1, hi, send_cache)
        else:
            each(lo, hi, send_cache)

    loads[2].wait()

    def send_text(step):
        push(text_raw.at[:, :, columns(step)], text_buf.at[seq], send_sem.at[2], recv_sem.at[2], target(step))

    each_remote(send_text)
    pltpu.make_async_copy(text_raw.at[:, :, columns(SELF)], text_buf.at[seq], recv_sem.at[2]).start()

    loads[1].wait()
    large = split_matrix(TOK * 2)

    def stage_kv(step):
        mixed = kv_raw[:, :, columns(step)].reshape(TOK * 2, HEAD)
        kv_stage[step] = split_rows(large, mixed).reshape(2, TOK, HEAD)

    def send_kv(step, kind):
        push(kv_stage.at[step, kind], kv_buf.at[kind, rows(step), :], send_sem.at[1], recv_kv.at[kind], target(step))

    def send_keys(step):
        stage_kv(step)
        send_kv(step, 0)

    each_remote(send_keys)
    stage_kv(SELF)
    for kind in range(2):
        pltpu.make_async_copy(
            kv_stage.at[SELF, kind], kv_buf.at[kind, rows(SELF), :], recv_kv.at[kind]
        ).start()
    each_remote(lambda step: send_kv(step, 1))

    for part in range(PARTS):
        await_bytes(pools[part].at[0], recv_c.at[part])
        for shift in range(1, NY):
            push(pools[part].at[0], pools[part].at[shift], send_y.at[part], recv_y.at[part], y_target(shift))

    each(8, SEQ, send_q)

    def entry(clip, w):
        slot = slots[ids[w, clip]]
        owner = slot // OWN
        return owner // NY, (y - owner % NY + NY) % NY, slot % OWN

    partner = (1 - x_hi) * NY + y
    for part in range(PARTS):
        await_bytes(pools[part].at[pl.ds(1, NY - 1)], recv_y.at[part])
        for w in range(WINDOW):
            _, shift, slot = entry(partner, w)
            gives[part][w] = pools[part][shift, :, slot]
        push(gives[part], gots[part], send_x.at[part], recv_x.at[part], x_target)

    for part in range(PARTS):
        await_bytes(gots[part], recv_x.at[part])
        for w in range(WINDOW):
            side, shift, slot = entry(group, w)
            here = jnp.full((2, PART, HEAD), side, jnp.int32) == x_hi
            near = pools[part][shift, :, slot].astype(F32)
            far = gots[part][w].astype(F32)
            window[w, :, part * PART : (part + 1) * PART, :] = jnp.where(here, near, far).astype(BF16)

    await_bytes(text_buf, recv_sem.at[2])
    for half in range(2):
        mixed = text_buf[half * 16 : (half + 1) * 16].reshape(TEXT, HEAD)
        text_kv[:, half * 128 : (half + 1) * 128, :] = split_rows(large, mixed).reshape(2, 128, HEAD)

    await_bytes(kv_buf.at[0], recv_kv.at[0])

    live = counts[group]
    biases = [jnp.where(w < live, 0.0, DEAD).astype(F32) for w in range(WINDOW)]
    text_live = lax.broadcasted_iota(jnp.int32, (ROWS, TEXT), 1) < text_counts[group]
    tiles = [(kv_buf.at[0, pl.ds(j * TILE, TILE)], kv_buf.at[1, pl.ds(j * TILE, TILE)], None) for j in range(KEYS // TILE)]
    tiles += [(window.at[w, 0], window.at[w, 1], biases[w]) for w in range(WINDOW)]

    def fold(op, wide):
        part = wide[:, 0:HEAD]
        for u in range(1, wide.shape[1] // HEAD):
            part = op(part, wide[:, u * HEAD : (u + 1) * HEAD])
        return part

    def score(q_rows, keys):
        return lax.dot_general(q_rows, keys, (((1,), (1,)), ((), ())), preferred_element_type=F32)

    ones = jnp.ones((TILE, HEAD), BF16)

    def begin(chunk):
        return q_buf[pl.ds(pl.multiple_of(chunk * ROWS, ROWS), ROWS), :]

    def first_tile(q_rows, side, j, top):
        keys, _, bias = tiles[j]
        s = score(q_rows, keys[...])
        scores[side, :, j * TILE : (j + 1) * TILE] = s
        peak = fold(jnp.maximum, s)
        if bias is not None:
            peak = peak + bias
        return peak if top is None else jnp.maximum(top, peak)

    def first_end(q_rows, side, top):
        s = jnp.where(text_live, score(q_rows, text_kv[0]), DEAD)
        scores[side, :, SPAN : SPAN + TEXT] = s
        text_top = jnp.max(fold(jnp.maximum, s), axis=1, keepdims=True)
        return jnp.max(top, axis=1, keepdims=True), text_top

    def second_tile(side, j, top, mixed):
        _, values, bias = tiles[j]
        shift = top if bias is None else top - bias
        w = jnp.exp2((scores[side, :, j * TILE : (j + 1) * TILE] - shift) * F32(EXP_SCALE))
        both = jnp.concatenate([values[...], ones], axis=1)
        return mixed + jnp.dot(w.astype(BF16), both, preferred_element_type=F32)

    def second_end(chunk, side, text_top, mixed):
        w = jnp.exp2((scores[side, :, SPAN : SPAN + TEXT] - text_top) * F32(EXP_SCALE))
        text_total = jnp.sum(fold(jnp.add, w), axis=1, keepdims=True)
        text_mixed = jnp.dot(w.astype(BF16), text_kv[1], preferred_element_type=F32)
        result = mixed[:, :HEAD] / mixed[:, HEAD:] + text_mixed / text_total
        result = result * F32(SEND_SCALE)
        result = (result * result) * (result * jnp.abs(result))
        o_buf[pl.ds(pl.multiple_of(chunk * ROWS, ROWS), ROWS), :] = result.astype(BF16)

    def advance(chunk, side, tops, follow=True):
        q_rows = begin(chunk + 1) if follow else None
        mixed = jnp.zeros((ROWS, 2 * HEAD), F32)
        top = None
        for j in range(len(tiles)):
            if follow:
                top = first_tile(q_rows, 1 - side, j, top)
            mixed = second_tile(side, j, tops[0], mixed)
        after = first_end(q_rows, 1 - side, top) if follow else None
        second_end(chunk, side, tops[1], mixed)
        return after

    my_columns = pl.ds(pl.multiple_of(head_of(z, x_lo, core) * HEAD, HEAD), HEAD)

    def send_o(step):
        push(o_buf.at[rows(step), :], out_hbm.at[:, my_columns], send_sem.at[4], recv_sem.at[4], target(step, -1))

    def q_ready(chunk):
        await_bytes(q_buf.at[pl.ds(pl.multiple_of(chunk * ROWS, ROWS), ROWS), :], recv_q.at[chunk])

    q_ready(0)
    q_rows = begin(0)
    top = None
    for j in range(len(tiles)):
        top = first_tile(q_rows, 0, j, top)
    tops = first_end(q_rows, 0, top)

    def send_chunk(chunk):
        own = jnp.where(chunk == SELF // 4, 1, 0)
        each(4 * chunk + own, 4 * chunk + 4, send_o)

        @pl.when(chunk == SELF // 4)
        def _():
            pltpu.make_async_copy(o_buf.at[rows(SELF), :], out_hbm.at[:, my_columns], recv_sem.at[4]).start()

    def pair(h, tops):
        for side in range(2):
            chunk = 2 * h + side
            q_ready(chunk + 1)
            tops = advance(chunk, side, tops)
            send_chunk(chunk)
        return tops

    await_bytes(kv_buf.at[1], recv_kv.at[1])
    tops = lax.fori_loop(0, CHUNKS // 2 - 1, pair, tops)
    q_ready(CHUNKS - 1)
    tops = advance(CHUNKS - 2, 0, tops)
    each(4 * (CHUNKS - 2), 4 * (CHUNKS - 1), send_o)
    advance(CHUNKS - 1, 1, tops, follow=False)
    each(4 * (CHUNKS - 1), SEQ, send_o)

    others = pl.ds(0, SEQ - 1)
    await_bytes(cache_stage.at[others], send_sem.at[0])
    await_bytes(kv_stage.at[others], send_sem.at[1])
    await_bytes(text_buf.at[others], send_sem.at[2])
    await_bytes(q_buf.at[pl.ds(0, (SEQ - 1) * TOK), :], send_sem.at[3])
    for part in range(PARTS):
        await_bytes(pools[part].at[pl.ds(1, NY - 1)], send_y.at[part])
        await_bytes(gives[part], send_x.at[part])
    await_bytes(o_buf.at[pl.ds(0, (SEQ - 1) * TOK), :], send_sem.at[4])
    await_bytes(out_hbm, recv_sem.at[4])


def decode(coded_hbm, out_hbm, coded, out, load_sem, store_sem):
    loads, stores = [], []
    for i in range(PIECES):
        at = pl.ds(i * PIECE, PIECE)
        loads.append(pltpu.make_async_copy(coded_hbm.at[at], coded.at[i], load_sem.at[i]))
        stores.append(pltpu.make_async_copy(out.at[i], out_hbm.at[at], store_sem.at[i]))
    for load in loads:
        load.start()
    for i in range(PIECES):
        loads[i].wait()
        power = coded[i].astype(F32)
        size = lax.rsqrt(lax.rsqrt(jnp.abs(power))) * F32(1.0 / SEND_SCALE)
        size = jnp.where(power == 0.0, 0.0, size)
        out[i] = jnp.where(power < 0.0, -size, size)
        stores[i].start()
    for store in stores:
        store.wait()


def on_device(queries, current_kv, text_kv, cache_kv, window_ids, window_count, cache_slot, text_count):
    tok, width = queries.shape[1], queries.shape[2]
    hbm = pl.BlockSpec(memory_space=pl.ANY)
    smem = pl.BlockSpec(memory_space=pltpu.SMEM)
    vmem = pltpu.VMEM
    dma = pltpu.SemaphoreType.DMA
    coded = pl.pallas_call(
        body,
        out_shape=jax.ShapeDtypeStruct((tok, width), BF16),
        in_specs=[hbm] * 4 + [smem] * 4,
        out_specs=hbm,
        scratch_shapes=[
            vmem((tok, width), BF16),
            vmem((tok, 2, width), BF16),
            vmem((TTOK, 2, width), BF16),
            vmem((OWN, CTOK, 2, width), BF16),
            vmem((SEQ, 2, TOK, HEAD), BF16),
            vmem((SEQ, 2, OWN, CTOK, HEAD), BF16),
            vmem((KEYS, HEAD), BF16),
            vmem((2, KEYS, HEAD), BF16),
            vmem((SEQ, TTOK, 2, HEAD), BF16),
            vmem((2, TEXT, HEAD), BF16),
        ]
        + [vmem((NY, 2, OWN, PART, HEAD), BF16)] * PARTS
        + [vmem((WINDOW, 2, PART, HEAD), BF16)] * (2 * PARTS)
        + [
            vmem((WINDOW, 2, CACHE, HEAD), BF16),
            vmem((2, ROWS, SPAN + TEXT), F32),
            vmem((KEYS, HEAD), BF16),
            dma((4,)),
            dma((5,)),
            dma((PARTS,)),
            dma((PARTS,)),
            dma((5,)),
            dma((2,)),
            dma((CHUNKS,)),
            dma((PARTS,)),
            dma((PARTS,)),
            dma((PARTS,)),
        ],
        compiler_params=pltpu.CompilerParams(
            collective_id=0, has_side_effects=True, vmem_limit_bytes=58 * 2**20
        ),
        name="attention",
    )(
        queries[0], current_kv[0], text_kv[0], cache_kv,
        window_ids.T, window_count, cache_slot, text_count,
    )
    return pl.pallas_call(
        decode,
        out_shape=jax.ShapeDtypeStruct((tok, width), F32),
        in_specs=[hbm],
        out_specs=hbm,
        scratch_shapes=[
            vmem((PIECES, PIECE, width), BF16),
            vmem((PIECES, PIECE, width), F32),
            dma((PIECES,)),
            dma((PIECES,)),
        ],
        compiler_params=pltpu.CompilerParams(vmem_limit_bytes=58 * 2**20),
        name="decode",
    )(coded).reshape(1, tok, width)


def solution(mesh):
    return jax.shard_map(
        on_device,
        mesh=mesh,
        in_specs=(
            P("group", "seq", None),
            P("group", "seq", None, None),
            P("group", "seq", None, None),
            P("group", "seq", None, None),
            P(),
            P(),
            P(),
            P(),
        ),
        out_specs=P("group", "seq", None),
        check_vma=False,
    )
```
